32 devices in a mesh: region: 8 (over y, x, core), shard: 4 (over z).
Axes of the slice: x: 2, y: 2, z: 4, core: 2. Of those that a mesh axis runs over, the one named last changes fastest.
Arguments:
- planes: bfloat16 [4, 1024, 512], P(None, ('region', 'shard')), may hold values from -6 to 6
- sed_weights: float32 [6, 4], replicated, may hold values from 0.1 to 2
- psf_taps: float32 [2, 6, 3, 25], replicated, may hold values from 0.004 to 0.08
- resample_rows: bfloat16 [1024, 128, 128], P(('region', 'shard')), may hold values from -0.5 to 0.5
- resample_cols: bfloat16 [1024, 128, 256], P(('region', 'shard')), may hold values from -0.375 to 0.375
- observed: bfloat16 [1024, 128, 128], P(('region', 'shard')), may hold values from -6 to 6
- exposure_meta: int32 [3, 1024], P(None, 'region'), may hold values from 0 to 5, as said below
- slot_counts: int32 [8, 4], P('region'), may hold values from 8 to 32, as said below
Outputs:
- plane_grad: float32 [4, 1024, 512], P(None, ('region', 'shard'))
The draws below stay inside these ranges and needn't reach their ends.
Inputs may be any that keep to these rules, and one draw needn't show every extreme that they name: `exposure_meta`: row 0 is a row tile of the exposure's region, 0 to 3; row 1 a column tile, 0 to 1; row 2 a band, 0 to 5. `slot_counts`: the live slots of a device are its first ones. In every region one device has all 32 slots live, the others between 8 and 16.
All inputs are finite; a program needn't handle non-finite values.
Results may differ from the reference program's by a relative error of at most 0.003.
Values may be sent and summed in bfloat16 or wider, within the bound.
No kernel may reach another device: no remote copies, remote signals or barrier semaphores. Data moves between devices by JAX's collectives and lax.ppermute only.
A program may use at most 64 MiB of HBM per device.

```python
import math
import jax
import jax.numpy as jnp
from jax import lax

COMPONENTS = 4
BANDS = 6
TERMS = 3
TAPS = 25
TILE_ROWS = 32
COLS = 512
WIN_Y = 128
WIN_X = 256
OUT = 128
E_SLOT = 32
REGIONS = 8
SHARDS = 4
ROWS = 1024
EXPOSURES = 1024
N_SHARD = 4


def draw_exposure_meta(key, part):
    row_tile = jax.random.randint(jax.random.fold_in(key, 11), (EXPOSURES,), 0, SHARDS)
    col_tile = jax.random.randint(jax.random.fold_in(key, 12), (EXPOSURES,), 0, COLS // WIN_X)
    band = jax.random.randint(jax.random.fold_in(key, 13), (EXPOSURES,), 0, BANDS)
    return jnp.stack([row_tile, col_tile, band]).astype(jnp.int32)


def draw_slot_counts(key, part):
    base = jax.random.randint(jax.random.fold_in(key, 21), (REGIONS, SHARDS), E_SLOT // 4, E_SLOT // 2 + 1)
    full = jax.random.randint(jax.random.fold_in(key, 22), (REGIONS,), 0, SHARDS)
    column = jnp.arange(SHARDS, dtype=jnp.int32)[None, :]
    return jnp.where(column == full[:, None], E_SLOT, base).astype(jnp.int32)


def shard_levels(stream_key, dims, pieces, low, top_value):
    factor_of, own = 1.0, jax.random.fold_in(stream_key, 6)
    for axis_at, shards_of in pieces:
        steps = jnp.exp(jax.random.uniform(jax.random.fold_in(own, axis_at), (shards_of,), jnp.float32, low / len(pieces), top_value / len(pieces)))
        factor_of = factor_of * jnp.repeat(steps, dims[axis_at] // shards_of).reshape([-1 if axis == axis_at else 1 for axis in range(len(dims))])
    return factor_of


def centred(rng, extent, spread, most, cuts=(), kind=jnp.bfloat16):
    result = spread * jax.random.normal(rng, extent, jnp.float32)
    if cuts:
        result = result * shard_levels(rng, extent, cuts, -0.22, 0.18)
    return jnp.clip(result, -most, most).astype(kind)


def setup_inputs(seed: int = 0) -> dict:
    key_list = jax.random.split(jax.random.key(seed), 9)
    return {
        "planes": centred(key_list[0], (COMPONENTS, ROWS, COLS), 1.0, 6.0, ((1, 32),)),
        "sed_weights": jnp.clip(jnp.exp(jax.random.uniform(key_list[1], (BANDS, COMPONENTS), jnp.float32, math.log(0.1), math.log(2.0))), 0.1, 2.0),
        "psf_taps": jnp.clip(jnp.exp(jax.random.uniform(key_list[2], (2, BANDS, TERMS, TAPS), jnp.float32, math.log(0.004), math.log(0.08))), 0.004, 0.08),
        "resample_rows": centred(key_list[3], (EXPOSURES, OUT, WIN_Y), WIN_Y ** -0.5, 0.5, ((0, 32),)),
        "resample_cols": centred(key_list[4], (EXPOSURES, OUT, WIN_X), WIN_X ** -0.5, 0.375, ((0, 32),)),
        "observed": centred(key_list[5], (EXPOSURES, OUT, OUT), 1.0, 6.0, ((0, 32),)),
        "exposure_meta": draw_exposure_meta(jax.random.fold_in(key_list[8], 71), 0),
        "slot_counts": draw_slot_counts(jax.random.fold_in(key_list[8], 71), 0),
    }


def settle(value):
    return lax.optimization_barrier(value.astype(jnp.bfloat16)).astype(jnp.float32)


def band_tables(taps, width):
    tap_count = taps.shape[-1]
    offset = jnp.arange(width, dtype=jnp.int32)[:, None] - jnp.arange(width, dtype=jnp.int32)[None, :] + tap_count // 2
    selector = (offset[None, :, :] == jnp.arange(tap_count, dtype=jnp.int32)[:, None, None]).astype(jnp.float32)
    return jnp.einsum("btk,kij->btij", taps.astype(jnp.float32), selector, precision=lax.Precision.HIGHEST).astype(jnp.bfloat16)


def exposure_gradient(window, sed_row, rows_band, cols_band, row_map, col_map, pixels):
    py_mat = rows_band.astype(jnp.float32)
    px_mat = cols_band.astype(jnp.float32)
    ry_mat = row_map.astype(jnp.float32)
    rx_mat = col_map.astype(jnp.float32)
    mixed = settle(jnp.sum(sed_row[:, None, None] * window, axis=0))
    smeared = settle(jnp.einsum("tiy,yx->tix", py_mat, mixed))
    blurred = settle(jnp.einsum("tix,tjx->ij", smeared, px_mat))
    sampled = settle(jnp.einsum("oy,yx->ox", ry_mat, blurred))
    model = jnp.einsum("ox,px->op", sampled, rx_mat)
    misfit = settle(model - pixels.astype(jnp.float32))
    back_rows = settle(jnp.einsum("oy,op->yp", ry_mat, misfit))
    back = settle(jnp.einsum("yp,px->yx", back_rows, rx_mat))
    unsmeared = settle(jnp.einsum("tiy,ix->tyx", py_mat, back))
    return jnp.einsum("tyj,tjx->yx", unsmeared, px_mat)


def reference(planes, sed_weights, psf_taps, resample_rows, resample_cols, observed, exposure_meta, slot_counts):
    region_rows = TILE_ROWS * N_SHARD
    rim_rows = WIN_Y - TILE_ROWS
    padded = jnp.concatenate([planes, jnp.zeros((COMPONENTS, rim_rows, COLS), planes.dtype)], axis=1)
    rows_tab = band_tables(psf_taps[0], WIN_Y)
    cols_tab = band_tables(psf_taps[1], WIN_X)
    per_region = N_SHARD * E_SLOT

    def visit(gradient, slot):
        region = slot // per_region
        device = (slot % per_region) // E_SLOT
        local = slot % E_SLOT
        count = slot_counts[region, device]

        def work(current):
            row_start = (region * region_rows + exposure_meta[0, slot] * TILE_ROWS).astype(jnp.int32)
            col_start = (exposure_meta[1, slot] * WIN_X).astype(jnp.int32)
            band = exposure_meta[2, slot]
            zero = jnp.zeros((), jnp.int32)
            window = lax.dynamic_slice(padded, (zero, row_start, col_start), (COMPONENTS, WIN_Y, WIN_X)).astype(jnp.float32)
            sed_row = sed_weights[band]
            window_grad = exposure_gradient(window, sed_row, rows_tab[band], cols_tab[band], resample_rows[slot], resample_cols[slot], observed[slot])
            part = lax.dynamic_slice(current, (zero, row_start, col_start), (COMPONENTS, WIN_Y, WIN_X))
            return lax.dynamic_update_slice(current, part + sed_row[:, None, None] * window_grad[None], (zero, row_start, col_start))

        return lax.cond(local < count, work, lambda current: current, gradient), None

    start = jnp.zeros((COMPONENTS, ROWS + rim_rows, COLS), jnp.float32)
    gradient, _ = lax.scan(visit, start, jnp.arange(EXPOSURES, dtype=jnp.int32))
    return gradient[:, :ROWS]
```

```python
import functools

import jax
import jax.numpy as jnp
from jax import lax
from jax.experimental import pallas as pl
from jax.experimental.pallas import tpu as pltpu
from jax.sharding import PartitionSpec as P

GROUP = 4


def shifted(block, axis, distance):
    size = lax.axis_size(axis)
    return lax.ppermute(block, axis, [(i, (i + distance) % size) for i in range(size)])


def passed_along(block, axis, distance):
    devices = range(lax.axis_size(axis))
    route = [(i - distance, i) for i in devices if i - distance in devices]
    return lax.ppermute(block, axis, route)


def band_tables(taps, width):
    tap_count = taps.shape[-1]
    offset = (
        jnp.arange(width, dtype=jnp.int32)[:, None]
        - jnp.arange(width, dtype=jnp.int32)[None, :]
        + tap_count // 2
    )
    selector = (offset[None, :, :] == jnp.arange(tap_count, dtype=jnp.int32)[:, None, None]).astype(
        jnp.float32
    )
    table = jnp.einsum("btk,kij->btij", taps, selector, precision=lax.Precision.HIGHEST)
    bands, terms = taps.shape[:2]
    return table.astype(jnp.bfloat16).reshape(bands, terms * width, width)


def dot(a, b, contract):
    return lax.dot_general(a, b, ((contract[:1], contract[1:]), ((), ())), preferred_element_type=jnp.float32)


def exposures_kernel(
    terms,
    tile_rows,
    count_ref,
    row_tile_ref,
    col_tile_ref,
    band_ref,
    sed_ref,
    ext_ref,
    py_ref,
    py_t_ref,
    px_ref,
    px_t_ref,
    ry_hbm,
    rx_hbm,
    obs_hbm,
    grad_ref,
    ry_ref,
    rx_ref,
    obs_ref,
    sems,
):
    channels, ext_rows, cols = ext_ref.shape
    slots, out_rows, win_rows = ry_hbm.shape
    win_cols = rx_hbm.shape[2]
    count = count_ref[0]
    turns = (count + GROUP - 1) // GROUP

    def copies(slot):
        return [
            pltpu.make_async_copy(hbm.at[slot], vmem.at[slot], sems.at[i, slot])
            for i, (hbm, vmem) in enumerate(((ry_hbm, ry_ref), (rx_hbm, rx_ref), (obs_hbm, obs_ref)))
        ]

    def fetch(slot, carry):
        for copy in copies(slot):
            copy.start()
        return carry

    lax.fori_loop(0, turns * GROUP, fetch, 0)
    grad_ref[...] = jnp.zeros_like(grad_ref)

    def visit(turn, carry):
        slot_of = [turn * GROUP + m for m in range(GROUP)]
        band = [band_ref[s] for s in slot_of]
        row = [pl.multiple_of(row_tile_ref[s] * tile_rows, tile_rows) for s in slot_of]
        col = [pl.multiple_of(col_tile_ref[s] * win_cols, win_cols) for s in slot_of]
        live = [(s < count).astype(jnp.float32) for s in slot_of]
        weight = [[sed_ref[b, k] for k in range(channels)] for b in band]
        for s in slot_of:
            for copy in copies(s):
                copy.wait()
        mixed = []
        for m in range(GROUP):
            total = None
            for k in range(channels):
                window = ext_ref[k, pl.ds(row[m], win_rows), pl.ds(col[m], win_cols)]
                term = weight[m][k] * window.astype(jnp.float32)
                total = term if total is None else total + term
            mixed.append(total.astype(jnp.bfloat16))
        smeared = [dot(py_ref[band[m]], mixed[m], (1, 0)).astype(jnp.bfloat16) for m in range(GROUP)]
        blurred = []
        for m in range(GROUP):
            wide = jnp.concatenate([smeared[m][t * win_rows : (t + 1) * win_rows] for t in range(terms)], axis=1)
            blurred.append(dot(wide, px_t_ref[band[m]], (1, 0)).astype(jnp.bfloat16))
        sampled = [dot(ry_ref[slot_of[m]], blurred[m], (1, 0)).astype(jnp.bfloat16) for m in range(GROUP)]
        model = [dot(sampled[m], rx_ref[slot_of[m]], (1, 1)) for m in range(GROUP)]
        misfit = [
            (model[m] - obs_ref[slot_of[m]].astype(jnp.float32)).astype(jnp.bfloat16) for m in range(GROUP)
        ]
        back_rows = [dot(ry_ref[slot_of[m]], misfit[m], (0, 0)).astype(jnp.bfloat16) for m in range(GROUP)]
        back = [dot(back_rows[m], rx_ref[slot_of[m]], (1, 0)).astype(jnp.bfloat16) for m in range(GROUP)]
        unsmeared = [dot(py_t_ref[band[m]], back[m], (1, 0)).astype(jnp.bfloat16) for m in range(GROUP)]
        for m in range(GROUP):
            wide = jnp.concatenate([unsmeared[m][t * win_rows : (t + 1) * win_rows] for t in range(terms)], axis=1)
            window_grad = dot(wide, px_ref[band[m]], (1, 0))
            for k in range(channels):
                place = (k, pl.ds(row[m], win_rows), pl.ds(col[m], win_cols))
                grad_ref[place] = grad_ref[place] + (weight[m][k] * live[m]) * window_grad
        return carry

    lax.fori_loop(0, turns, visit, 0)


def local(
    planes,
    sed_weights,
    psf_taps,
    resample_rows,
    resample_cols,
    observed,
    exposure_meta,
    slot_counts,
):
    shard_count = lax.axis_size("shard")
    my_index = lax.axis_index("shard")
    channel_count, tile_rows, col_total = planes.shape
    slot_count, out_rows, win_rows = resample_rows.shape
    win_cols = resample_cols.shape[2]
    region_rows = tile_rows * shard_count
    rim_rows = win_rows - tile_rows
    terms = psf_taps.shape[2]
    gathered = lax.all_gather(planes, "shard", axis=1, tiled=True)
    next_part = passed_along(gathered[:, :rim_rows], "region", -1)
    extended = jnp.concatenate([gathered, next_part], axis=1)
    py = band_tables(psf_taps[0], win_rows)
    py_t = band_tables(psf_taps[0, :, :, ::-1], win_rows)
    px = band_tables(psf_taps[1], win_cols)
    px_t = band_tables(psf_taps[1, :, :, ::-1], win_cols)
    count = lax.dynamic_slice(slot_counts[0], (my_index,), (1,))
    meta = lax.dynamic_slice(exposure_meta, (jnp.int32(0), my_index * slot_count), (3, slot_count))

    smem = pl.BlockSpec(memory_space=pltpu.SMEM)
    vmem = pl.BlockSpec(memory_space=pltpu.VMEM)
    anywhere = pl.BlockSpec(memory_space=pl.ANY)
    gradient = pl.pallas_call(
        functools.partial(exposures_kernel, terms, tile_rows),
        out_shape=jax.ShapeDtypeStruct((channel_count, region_rows + rim_rows, col_total), jnp.float32),
        in_specs=[smem] * 5 + [vmem] * 5 + [anywhere] * 3,
        out_specs=vmem,
        scratch_shapes=[
            pltpu.VMEM((slot_count, out_rows, win_rows), jnp.bfloat16),
            pltpu.VMEM((slot_count, out_rows, win_cols), jnp.bfloat16),
            pltpu.VMEM((slot_count, out_rows, out_rows), jnp.bfloat16),
            pltpu.SemaphoreType.DMA((3, slot_count)),
        ],
        compiler_params=pltpu.CompilerParams(vmem_limit_bytes=48 * 1024 * 1024),
        cost_estimate=pl.CostEstimate(flops=6 * 10**9, bytes_accessed=6 * 10**6, transcendentals=0),
    )(
        count,
        meta[0],
        meta[1],
        meta[2],
        sed_weights,
        extended,
        py,
        py_t,
        px,
        px_t,
        resample_rows,
        resample_cols,
        observed,
    )

    spill = passed_along(gradient[:, region_rows:].astype(jnp.bfloat16), "region", 1)
    own_rows = gradient[:, :region_rows].at[:, :rim_rows].add(spill.astype(jnp.float32))
    result = lax.dynamic_slice(own_rows, (jnp.int32(0), my_index * tile_rows, jnp.int32(0)), planes.shape)
    for step in range(1, shard_count):
        there = lax.rem(my_index + step, shard_count) * tile_rows
        part = lax.dynamic_slice(own_rows, (jnp.int32(0), there, jnp.int32(0)), planes.shape)
        result = result + shifted(part.astype(jnp.bfloat16), "shard", step).astype(jnp.float32)
    return result


def solution(mesh):
    placed = (
        P(None, ("region", "shard"), None),
        P(),
        P(),
        P(("region", "shard"), None, None),
        P(("region", "shard"), None, None),
        P(("region", "shard"), None, None),
        P(None, "region"),
        P("region", None),
    )
    return jax.shard_map(
        local,
        mesh=mesh,
        in_specs=placed,
        out_specs=P(None, ("region", "shard"), None),
        check_vma=False,
    )
```

```python
import functools

import jax
import jax.numpy as jnp
from jax import lax
from jax.experimental import pallas as pl
from jax.experimental.pallas import tpu as pltpu
from jax.sharding import PartitionSpec as P

GROUPS = (8, 4, 2)
ROW_ALIGN = 32
VMEM_LIMIT = 16 * 1024 * 1024
SMALL_VMEM_LIMIT = 4 * 1024 * 1024


def shifted(block, axis, distance):
    size = lax.axis_size(axis)
    return lax.ppermute(block, axis, [(i, (i + distance) % size) for i in range(size)])


def passed_along(block, axis, distance):
    devices = range(lax.axis_size(axis))
    route = [(i - distance, i) for i in devices if i - distance in devices]
    return lax.ppermute(block, axis, route)


def dot(a, b, contract):
    return lax.dot_general(a, b, ((contract[:1], contract[1:]), ((), ())), preferred_element_type=jnp.float32)


def prepare_kernel(
    tile_rows,
    taps_hbm,
    sed_hbm,
    meta_hbm,
    counts_hbm,
    ry_hbm,
    rx_hbm,
    obs_hbm,
    py_ref,
    py_t_ref,
    px_ref,
    px_t_ref,
    ry_ref,
    rx_ref,
    obs_ref,
    sed_ref,
    *rest,
):
    plans, (taps_ref, lines_ref, meta_ref, counts_ref, sems) = rest[:-5], rest[-5:]
    bands, terms, axes, tap_count = taps_ref.shape
    slots = ry_ref.shape[0]
    half = tap_count // 2
    moves = [
        pltpu.make_async_copy(source, target, sems.at[i])
        for i, (source, target) in enumerate(
            (
                (taps_hbm, taps_ref),
                (meta_hbm, meta_ref),
                (counts_hbm, counts_ref),
                (sed_hbm, sed_ref),
                (ry_hbm, ry_ref),
                (rx_hbm, rx_ref),
                (obs_hbm, obs_ref),
            )
        )
    ]
    for move in moves:
        move.start()
    lines_ref[...] = jnp.zeros_like(lines_ref)
    lanes = lines_ref.shape[2]
    mirror = lax.broadcasted_iota(jnp.int32, (lanes, lanes), 0) + lax.broadcasted_iota(jnp.int32, (lanes, lanes), 1)
    mirror = (mirror == tap_count - 1).astype(jnp.bfloat16)
    for move in moves[:3]:
        move.wait()

    def one_band(b, carry):
        for t in range(terms):
            lines_ref[b, axes * t : axes * (t + 1), :tap_count] = taps_ref[b, t]
        forward = lines_ref[b].astype(jnp.bfloat16)
        mirrored = dot(forward, mirror, (1, 0))
        forward = forward.astype(jnp.float32)
        for axis, (turned_ref, straight_ref) in enumerate(((py_ref, py_t_ref), (px_ref, px_t_ref))):
            width = straight_ref.shape[1]
            down = lax.broadcasted_iota(jnp.int32, (width, width), 0)
            right = lax.broadcasted_iota(jnp.int32, (width, width), 1)
            near = jnp.abs(down - right) <= half
            for lines, out_ref in ((forward, straight_ref), (mirrored, turned_ref)):
                if width > lanes:
                    lines = jnp.concatenate([lines, jnp.zeros((lines.shape[0], width - lanes), jnp.float32)], axis=1)
                centred = pltpu.roll(lines, width - half, 1)
                for t in range(terms):
                    line = centred[axes * t + axis : axes * t + axis + 1]
                    rolled = pltpu.roll(jnp.broadcast_to(line, (width, width)), 0, 1, stride=1, stride_axis=0)
                    table = jnp.where(near, rolled, 0.0)
                    out_ref[b, :, t * width : (t + 1) * width] = table.astype(jnp.bfloat16)
        return carry

    lax.fori_loop(0, bands, one_band, 0, unroll=True)

    mine = lax.axis_index("shard")

    def place(slot, found):
        at = mine * slots + slot
        col = meta_ref[1, at]
        after = []
        for c, plan_ref in enumerate(plans):
            hit = col == c
            plan_ref[1 + found[c]] = slot
            plan_ref[1 + slots + found[c]] = meta_ref[0, at] * tile_rows
            plan_ref[1 + 2 * slots + found[c]] = meta_ref[2, at]
            after.append(found[c] + hit.astype(jnp.int32))
        return tuple(after)

    found = lax.fori_loop(0, counts_ref[0, mine], place, (jnp.int32(0),) * len(plans))
    for plan_ref, total in zip(plans, found):
        plan_ref[0] = total
    for move in moves[3:]:
        move.wait()


def gather_kernel(*refs):
    tiles, (_, whole_ref, rim_ref) = refs[:-3], refs[-3:]
    count = len(tiles)
    tile_rows = tiles[0].shape[1]
    rim_tiles = rim_ref.shape[1] // tile_rows
    for k in range(count):
        owner = lax.rem(lax.axis_index("shard") + (count - k), count)
        place = pl.ds(pl.multiple_of(owner * tile_rows, tile_rows), tile_rows)
        whole_ref[:, place, :] = tiles[k][...]

        @pl.when(owner < rim_tiles)
        def _(place=place, tile=tiles[k]):
            rim_ref[:, place, :] = tile[...]


def exposures_kernel(
    terms,
    plan_ref,
    sed_ref,
    whole_ref,
    next_ref,
    py_ref,
    py_t_ref,
    px_ref,
    px_t_ref,
    ry_ref,
    rx_ref,
    obs_ref,
    own_ref,
    spill_ref,
    mix_ref,
    acc_ref,
):
    channels, bands = sed_ref.shape
    region_rows = whole_ref.shape[1]
    rim_rows = next_ref.shape[1]
    slots, _, win_rows = ry_ref.shape
    win_cols = rx_ref.shape[2]
    count = plan_ref[0]
    acc_ref[...] = jnp.zeros_like(acc_ref)

    def mix(b, carry):
        for part_ref, start in ((whole_ref, 0), (next_ref, region_rows)):
            total = None
            for k in range(channels):
                term = sed_ref[k, b] * part_ref[k].astype(jnp.float32)
                total = term if total is None else total + term
            mix_ref[b, start : start + part_ref.shape[1], :] = total.astype(jnp.bfloat16)
        return carry

    lax.fori_loop(0, bands, mix, 0)

    def visit(group, first):
        members = range(group)
        live = [first + m < count for m in members]
        rank = [jnp.minimum(first + m, count - 1) for m in members]
        slot_of = [plan_ref[1 + r] for r in rank]
        row = [pl.multiple_of(plan_ref[1 + slots + r], ROW_ALIGN) for r in rank]
        band = [plan_ref[1 + 2 * slots + r] for r in rank]
        mixed = [mix_ref[band[m], pl.ds(row[m], win_rows), :] for m in members]
        along = [dot(mixed[m], px_t_ref[band[m]], (1, 0)).astype(jnp.bfloat16) for m in members]
        stack = [
            jnp.concatenate([along[m][:, t * win_cols : (t + 1) * win_cols] for t in range(terms)], axis=0)
            for m in members
        ]
        blurred = [dot(py_ref[band[m]], stack[m], (1, 0)).astype(jnp.bfloat16) for m in members]
        sampled = [dot(ry_ref[slot_of[m]], blurred[m], (1, 0)).astype(jnp.bfloat16) for m in members]
        model = [dot(sampled[m], rx_ref[slot_of[m]], (1, 1)) for m in members]
        misfit = [(model[m] - obs_ref[slot_of[m]].astype(jnp.float32)).astype(jnp.bfloat16) for m in members]
        back_rows = [dot(ry_ref[slot_of[m]], misfit[m], (0, 0)).astype(jnp.bfloat16) for m in members]
        back = [dot(back_rows[m], rx_ref[slot_of[m]], (1, 0)).astype(jnp.bfloat16) for m in members]
        spread = [dot(back[m], px_ref[band[m]], (1, 0)).astype(jnp.bfloat16) for m in members]
        back_along = [
            jnp.concatenate([spread[m][:, t * win_cols : (t + 1) * win_cols] for t in range(terms)], axis=0)
            for m in members
        ]
        window_grad = [dot(py_t_ref[band[m]], back_along[m], (1, 0)) for m in members]
        for m in members:
            place = (band[m], pl.ds(row[m], win_rows), slice(None))
            acc_ref[place] = acc_ref[place] + jnp.where(live[m], window_grad[m], 0.0)

    done = jnp.int32(0)
    for at, group in enumerate(GROUPS):
        left = count - done
        turns = left // group if at < len(GROUPS) - 1 else (left + group - 1) // group

        def turn(i, carry, group=group, done=done):
            visit(group, done + i * group)
            return carry

        lax.fori_loop(0, turns, turn, 0)
        done = done + turns * group

    for k in range(channels):
        for out_ref, start, rows in ((spill_ref, region_rows, rim_rows), (own_ref, 0, region_rows)):
            total = None
            for b in range(bands):
                term = sed_ref[k, b] * acc_ref[b, start : start + rows, :]
                total = term if total is None else total + term
            out_ref[k] = total.astype(out_ref.dtype)


def share_kernel(own_ref, spilled_ref, kept_ref, *given):
    count = 1 + len(given)
    tile_rows = kept_ref.shape[1]
    rim_tiles = spilled_ref.shape[1] // tile_rows
    for k, out_ref in enumerate((kept_ref,) + given):
        owner = lax.rem(lax.axis_index("shard") + k, count)
        tile = own_ref[:, pl.ds(pl.multiple_of(owner * tile_rows, tile_rows), tile_rows), :]
        rim = pl.ds(pl.multiple_of(jnp.minimum(owner, rim_tiles - 1) * tile_rows, tile_rows), tile_rows)
        extra = jnp.where(owner < rim_tiles, spilled_ref[:, rim, :].astype(jnp.float32), 0.0)
        out_ref[...] = (tile + extra).astype(out_ref.dtype)


def local(
    planes,
    sed_weights,
    psf_taps,
    resample_rows,
    resample_cols,
    observed,
    exposure_meta,
    slot_counts,
):
    shard_count = lax.axis_size("shard")
    channel_count, tile_rows, col_total = planes.shape
    slot_count, out_rows, win_rows = resample_rows.shape
    win_cols = resample_cols.shape[2]
    col_tiles = col_total // win_cols
    region_rows = tile_rows * shard_count
    rim_rows = win_rows - tile_rows
    bands, terms, tap_count = psf_taps.shape[1:]
    smem = pl.BlockSpec(memory_space=pltpu.SMEM)
    vmem = pl.BlockSpec(memory_space=pltpu.VMEM)
    anywhere = pl.BlockSpec(memory_space=pl.ANY)
    tile_shape = (channel_count, tile_rows, win_cols)
    whole_shape = (channel_count, region_rows, win_cols)
    rim_shape = (channel_count, rim_rows, win_cols)

    tiles = []
    for c in range(col_tiles):
        own = planes[:, :, c * win_cols : (c + 1) * win_cols]
        tiles.append([own] + [shifted(own, "shard", k) for k in range(1, shard_count)])

    def spec(*shape):
        return jax.ShapeDtypeStruct(shape, jnp.bfloat16)

    prepared = pl.pallas_call(
        functools.partial(prepare_kernel, tile_rows),
        out_shape=(
            spec(bands, win_rows, terms * win_rows),
            spec(bands, win_rows, terms * win_rows),
            spec(bands, win_cols, terms * win_cols),
            spec(bands, win_cols, terms * win_cols),
            spec(*resample_rows.shape),
            spec(*resample_cols.shape),
            spec(*observed.shape),
            jax.ShapeDtypeStruct(sed_weights.shape[::-1], jnp.float32),
        )
        + (jax.ShapeDtypeStruct((1 + 3 * slot_count,), jnp.int32),) * col_tiles,
        in_specs=[anywhere] * 7,
        out_specs=(vmem,) * 7 + (smem,) * (1 + col_tiles),
        scratch_shapes=[
            pltpu.VMEM((bands, terms, 2, tap_count), jnp.float32),
            pltpu.VMEM((bands, 8 * ((2 * terms + 7) // 8), 128), jnp.float32),
            pltpu.SMEM(exposure_meta.shape, jnp.int32),
            pltpu.SMEM(slot_counts.shape, jnp.int32),
            pltpu.SemaphoreType.DMA((7,)),
        ],
        compiler_params=pltpu.CompilerParams(vmem_limit_bytes=VMEM_LIMIT),
        cost_estimate=pl.CostEstimate(flops=10**8, bytes_accessed=4 * 10**6, transcendentals=0),
    )(
        *(
            pltpu.with_memory_space_constraint(x, pltpu.HBM)
            for x in (
                psf_taps.transpose(1, 2, 0, 3),
                sed_weights.T,
                exposure_meta,
                slot_counts,
                resample_rows,
                resample_cols,
                observed,
            )
        )
    )
    plans = prepared[8:]

    result = []
    after = prepared[0]
    for c in range(col_tiles):
        whole, rim = pl.pallas_call(
            gather_kernel,
            out_shape=(
                jax.ShapeDtypeStruct(whole_shape, planes.dtype),
                jax.ShapeDtypeStruct(rim_shape, planes.dtype),
            ),
            in_specs=[vmem] * shard_count + [anywhere],
            out_specs=(vmem, vmem),
            compiler_params=pltpu.CompilerParams(vmem_limit_bytes=SMALL_VMEM_LIMIT),
            cost_estimate=pl.CostEstimate(flops=10**5, bytes_accessed=10**6, transcendentals=0),
        )(*tiles[c], after)
        following = passed_along(rim, "region", -1)
        own_rows, spill = pl.pallas_call(
            functools.partial(exposures_kernel, terms),
            out_shape=(
                jax.ShapeDtypeStruct(whole_shape, jnp.float32),
                jax.ShapeDtypeStruct(rim_shape, jnp.bfloat16),
            ),
            in_specs=[smem] * 2 + [vmem] * 9,
            out_specs=(vmem, vmem),
            scratch_shapes=[
                pltpu.VMEM((bands, region_rows + rim_rows, win_cols), jnp.bfloat16),
                pltpu.VMEM((bands, region_rows + rim_rows, win_cols), jnp.float32),
            ],
            compiler_params=pltpu.CompilerParams(vmem_limit_bytes=VMEM_LIMIT),
            cost_estimate=pl.CostEstimate(flops=6 * 10**9, bytes_accessed=6 * 10**6, transcendentals=0),
        )(plans[c], prepared[7], whole, following, *prepared[:7])
        after = own_rows
        spilled = passed_along(spill, "region", 1)
        total, *given = pl.pallas_call(
            share_kernel,
            out_shape=(jax.ShapeDtypeStruct(tile_shape, jnp.float32),)
            + (jax.ShapeDtypeStruct(tile_shape, jnp.bfloat16),) * (shard_count - 1),
            in_specs=[vmem] * 2,
            out_specs=(vmem,) * shard_count,
            compiler_params=pltpu.CompilerParams(vmem_limit_bytes=SMALL_VMEM_LIMIT),
            cost_estimate=pl.CostEstimate(flops=10**5, bytes_accessed=10**6, transcendentals=0),
        )(own_rows, spilled)
        for step in range(1, shard_count):
            total = total + shifted(given[step - 1], "shard", step).astype(jnp.float32)
        result.append(total)
    return jnp.concatenate(result, axis=2)


def solution(mesh):
    placed = (
        P(None, ("region", "shard"), None),
        P(),
        P(),
        P(("region", "shard"), None, None),
        P(("region", "shard"), None, None),
        P(("region", "shard"), None, None),
        P(None, "region"),
        P("region", None),
    )
    return jax.shard_map(
        local,
        mesh=mesh,
        in_specs=placed,
        out_specs=P(None, ("region", "shard"), None),
        check_vma=False,
    )
```

```python
import functools

import jax
import jax.numpy as jnp
from jax import lax
from jax.experimental import pallas as pl
from jax.experimental.pallas import tpu as pltpu
from jax.sharding import PartitionSpec as P

GROUPS = (12, 16, 20)
ROW_ALIGN = 32
ORDER_FLOPS = 10**10
VMEM_LIMIT = 16 * 1024 * 1024
SMALL_VMEM_LIMIT = 4 * 1024 * 1024


def shifted(block, axis, distance):
    size = lax.axis_size(axis)
    return lax.ppermute(block, axis, [(i, (i + distance) % size) for i in range(size)])


def passed_along(block, axis, distance):
    devices = range(lax.axis_size(axis))
    route = [(i - distance, i) for i in devices if i - distance in devices]
    return lax.ppermute(block, axis, route)


def dot(a, b, contract):
    return lax.dot_general(a, b, ((contract[:1], contract[1:]), ((), ())), preferred_element_type=jnp.float32)


def prepare_kernel(
    taps_hbm,
    ry_hbm,
    rx_hbm,
    obs_hbm,
    py_ref,
    py_t_ref,
    px_ref,
    px_t_ref,
    ry_ref,
    rx_ref,
    obs_ref,
    taps_ref,
    lines_ref,
    sems,
):
    bands, terms, axes, tap_count = taps_ref.shape
    half = tap_count // 2
    moves = [
        pltpu.make_async_copy(source, target, sems.at[i])
        for i, (source, target) in enumerate(
            (
                (taps_hbm, taps_ref),
                (ry_hbm, ry_ref),
                (rx_hbm, rx_ref),
                (obs_hbm, obs_ref),
            )
        )
    ]
    for move in moves:
        move.start()
    lines_ref[...] = jnp.zeros_like(lines_ref)
    lanes = lines_ref.shape[2]
    mirror = lax.broadcasted_iota(jnp.int32, (lanes, lanes), 0) + lax.broadcasted_iota(jnp.int32, (lanes, lanes), 1)
    mirror = (mirror == tap_count - 1).astype(jnp.bfloat16)
    moves[0].wait()

    def one_band(b, carry):
        for t in range(terms):
            lines_ref[b, axes * t : axes * (t + 1), :tap_count] = taps_ref[b, t]
        forward = lines_ref[b].astype(jnp.bfloat16)
        mirrored = dot(forward, mirror, (1, 0))
        forward = forward.astype(jnp.float32)
        for axis, (turned_ref, straight_ref) in enumerate(((py_ref, py_t_ref), (px_ref, px_t_ref))):
            width = straight_ref.shape[1]
            down = lax.broadcasted_iota(jnp.int32, (width, width), 0)
            right = lax.broadcasted_iota(jnp.int32, (width, width), 1)
            near = jnp.abs(down - right) <= half
            for lines, out_ref in ((forward, straight_ref), (mirrored, turned_ref)):
                if width > lanes:
                    lines = jnp.concatenate([lines, jnp.zeros((lines.shape[0], width - lanes), jnp.float32)], axis=1)
                centred = pltpu.roll(lines, width - half, 1)
                for t in range(terms):
                    line = centred[axes * t + axis : axes * t + axis + 1]
                    rolled = pltpu.roll(jnp.broadcast_to(line, (width, width)), 0, 1, stride=1, stride_axis=0)
                    table = jnp.where(near, rolled, 0.0)
                    out_ref[b, :, t * width : (t + 1) * width] = table.astype(jnp.bfloat16)
        return carry

    lax.fori_loop(0, bands, one_band, 0, unroll=True)
    for move in moves[1:]:
        move.wait()


def order_kernel(tile_rows, meta_hbm, counts_hbm, sed_hbm, _, sed_ref, *rest):
    plans, (meta_ref, counts_ref, sems) = rest[:-3], rest[-3:]
    slots = (plans[0].shape[0] - 1) // 3
    moves = [
        pltpu.make_async_copy(source, target, sems.at[i])
        for i, (source, target) in enumerate(((meta_hbm, meta_ref), (counts_hbm, counts_ref), (sed_hbm, sed_ref)))
    ]
    for move in moves:
        move.start()
    for move in moves:
        move.wait()
    mine = lax.axis_index("shard")

    def place(slot, found):
        at = mine * slots + slot
        col = meta_ref[1, at]
        after = []
        for c, plan_ref in enumerate(plans):
            plan_ref[1 + found[c]] = slot
            plan_ref[1 + slots + found[c]] = meta_ref[0, at] * tile_rows
            plan_ref[1 + 2 * slots + found[c]] = meta_ref[2, at]
            after.append(found[c] + (col == c).astype(jnp.int32))
        return tuple(after)

    found = lax.fori_loop(0, counts_ref[0, mine], place, (jnp.int32(0),) * len(plans))
    for plan_ref, total in zip(plans, found):
        plan_ref[0] = total


def gather_kernel(*refs):
    tiles, (_, whole_ref, rim_ref) = refs[:-3], refs[-3:]
    count = len(tiles)
    tile_rows = tiles[0].shape[1]
    rim_tiles = rim_ref.shape[1] // tile_rows
    for k in range(count):
        owner = lax.rem(lax.axis_index("shard") + (count - k), count)
        place = pl.ds(pl.multiple_of(owner * tile_rows, tile_rows), tile_rows)
        whole_ref[:, place, :] = tiles[k][...]

        @pl.when(owner < rim_tiles)
        def _(place=place, tile=tiles[k]):
            rim_ref[:, place, :] = tile[...]


def exposures_kernel(
    terms,
    plan_ref,
    sed_ref,
    whole_ref,
    next_ref,
    py_ref,
    py_t_ref,
    px_ref,
    px_t_ref,
    ry_ref,
    rx_ref,
    obs_ref,
    own_ref,
    spill_ref,
    mix_ref,
    acc_ref,
):
    channels, bands = sed_ref.shape
    region_rows = whole_ref.shape[1]
    rim_rows = next_ref.shape[1]
    slots, _, win_rows = ry_ref.shape
    win_cols = rx_ref.shape[2]
    count = plan_ref[0]
    acc_ref[...] = jnp.zeros_like(acc_ref)

    def mix(b, carry):
        for part_ref, start in ((whole_ref, 0), (next_ref, region_rows)):
            total = None
            for k in range(channels):
                term = sed_ref[k, b] * part_ref[k].astype(jnp.float32)
                total = term if total is None else total + term
            mix_ref[b, start : start + part_ref.shape[1], :] = total.astype(jnp.bfloat16)
        return carry

    lax.fori_loop(0, bands, mix, 0)

    def visit(group, first):
        members = range(group)
        live = [first + m < count for m in members]
        rank = [jnp.minimum(first + m, count - 1) for m in members]
        slot_of = [plan_ref[1 + r] for r in rank]
        row = [pl.multiple_of(plan_ref[1 + slots + r], ROW_ALIGN) for r in rank]
        band = [plan_ref[1 + 2 * slots + r] for r in rank]
        mixed = [mix_ref[band[m], pl.ds(row[m], win_rows), :] for m in members]
        along = [dot(mixed[m], px_t_ref[band[m]], (1, 0)).astype(jnp.bfloat16) for m in members]
        stack = [
            jnp.concatenate([along[m][:, t * win_cols : (t + 1) * win_cols] for t in range(terms)], axis=0)
            for m in members
        ]
        blurred = [dot(py_ref[band[m]], stack[m], (1, 0)).astype(jnp.bfloat16) for m in members]
        sampled = [dot(ry_ref[slot_of[m]], blurred[m], (1, 0)).astype(jnp.bfloat16) for m in members]
        model = [dot(sampled[m], rx_ref[slot_of[m]], (1, 1)) for m in members]
        misfit = [(model[m] - obs_ref[slot_of[m]].astype(jnp.float32)).astype(jnp.bfloat16) for m in members]
        back_rows = [dot(ry_ref[slot_of[m]], misfit[m], (0, 0)).astype(jnp.bfloat16) for m in members]
        back = [dot(back_rows[m], rx_ref[slot_of[m]], (1, 0)).astype(jnp.bfloat16) for m in members]
        spread = [dot(back[m], px_ref[band[m]], (1, 0)).astype(jnp.bfloat16) for m in members]
        back_along = [
            jnp.concatenate([spread[m][:, t * win_cols : (t + 1) * win_cols] for t in range(terms)], axis=0)
            for m in members
        ]
        window_grad = [dot(py_t_ref[band[m]], back_along[m], (1, 0)) for m in members]
        for m in members:
            place = (band[m], pl.ds(row[m], win_rows), slice(None))
            acc_ref[place] = acc_ref[place] + jnp.where(live[m], window_grad[m], 0.0)

    turns = (count + GROUPS[-1] - 1) // GROUPS[-1]
    fits = [turns * group >= count for group in GROUPS]
    for at, group in enumerate(GROUPS):
        taken = jnp.logical_and(fits[at], jnp.logical_not(fits[at - 1])) if at else fits[at]

        def turn(i, carry, group=group):
            visit(group, i * group)
            return carry

        lax.fori_loop(0, jnp.where(taken, turns, 0), turn, 0)

    for k in range(channels):
        for out_ref, start, rows in ((spill_ref, region_rows, rim_rows), (own_ref, 0, region_rows)):
            total = None
            for b in range(bands):
                term = sed_ref[k, b] * acc_ref[b, start : start + rows, :]
                total = term if total is None else total + term
            out_ref[k] = total.astype(out_ref.dtype)


def share_kernel(own_ref, spilled_ref, kept_ref, *given):
    count = 1 + len(given)
    tile_rows = kept_ref.shape[1]
    rim_tiles = spilled_ref.shape[1] // tile_rows
    for k, out_ref in enumerate((kept_ref,) + given):
        owner = lax.rem(lax.axis_index("shard") + k, count)
        tile = own_ref[:, pl.ds(pl.multiple_of(owner * tile_rows, tile_rows), tile_rows), :]
        rim = pl.ds(pl.multiple_of(jnp.minimum(owner, rim_tiles - 1) * tile_rows, tile_rows), tile_rows)
        extra = jnp.where(owner < rim_tiles, spilled_ref[:, rim, :].astype(jnp.float32), 0.0)
        out_ref[...] = (tile + extra).astype(out_ref.dtype)


def local(
    planes,
    sed_weights,
    psf_taps,
    resample_rows,
    resample_cols,
    observed,
    exposure_meta,
    slot_counts,
):
    shard_count = lax.axis_size("shard")
    channel_count, tile_rows, col_total = planes.shape
    slot_count, out_rows, win_rows = resample_rows.shape
    win_cols = resample_cols.shape[2]
    col_tiles = col_total // win_cols
    region_rows = tile_rows * shard_count
    rim_rows = win_rows - tile_rows
    bands, terms, tap_count = psf_taps.shape[1:]
    smem = pl.BlockSpec(memory_space=pltpu.SMEM)
    vmem = pl.BlockSpec(memory_space=pltpu.VMEM)
    anywhere = pl.BlockSpec(memory_space=pl.ANY)
    tile_shape = (channel_count, tile_rows, win_cols)
    whole_shape = (channel_count, region_rows, win_cols)
    rim_shape = (channel_count, rim_rows, win_cols)

    tiles = []
    for c in range(col_tiles):
        own = planes[:, :, c * win_cols : (c + 1) * win_cols]
        tiles.append([own] + [shifted(own, "shard", k) for k in range(1, shard_count)])

    def spec(*shape):
        return jax.ShapeDtypeStruct(shape, jnp.bfloat16)

    prepared = pl.pallas_call(
        prepare_kernel,
        out_shape=(
            spec(bands, win_rows, terms * win_rows),
            spec(bands, win_rows, terms * win_rows),
            spec(bands, win_cols, terms * win_cols),
            spec(bands, win_cols, terms * win_cols),
            spec(*resample_rows.shape),
            spec(*resample_cols.shape),
            spec(*observed.shape),
        ),
        in_specs=[anywhere] * 4,
        out_specs=(vmem,) * 7,
        scratch_shapes=[
            pltpu.VMEM((bands, terms, 2, tap_count), jnp.float32),
            pltpu.VMEM((bands, 8 * ((2 * terms + 7) // 8), 128), jnp.float32),
            pltpu.SemaphoreType.DMA((4,)),
        ],
        compiler_params=pltpu.CompilerParams(vmem_limit_bytes=VMEM_LIMIT),
        cost_estimate=pl.CostEstimate(flops=10**8, bytes_accessed=8 * 10**6, transcendentals=0),
    )(
        *(
            pltpu.with_memory_space_constraint(x, pltpu.HBM)
            for x in (psf_taps.transpose(1, 2, 0, 3), resample_rows, resample_cols, observed)
        )
    )

    result = []
    after = prepared[0]
    for c in range(col_tiles):
        whole, rim = pl.pallas_call(
            gather_kernel,
            out_shape=(
                jax.ShapeDtypeStruct(whole_shape, planes.dtype),
                jax.ShapeDtypeStruct(rim_shape, planes.dtype),
            ),
            in_specs=[vmem] * shard_count + [anywhere],
            out_specs=(vmem, vmem),
            compiler_params=pltpu.CompilerParams(vmem_limit_bytes=SMALL_VMEM_LIMIT),
            cost_estimate=pl.CostEstimate(flops=10**5, bytes_accessed=10**6, transcendentals=0),
        )(*tiles[c], after)
        following = passed_along(rim, "region", -1)
        if c == 0:
            sed, *plans = pl.pallas_call(
                functools.partial(order_kernel, tile_rows),
                out_shape=(jax.ShapeDtypeStruct(sed_weights.shape[::-1], jnp.float32),)
                + (jax.ShapeDtypeStruct((1 + 3 * slot_count,), jnp.int32),) * col_tiles,
                in_specs=[anywhere] * 4,
                out_specs=(smem,) * (1 + col_tiles),
                scratch_shapes=[
                    pltpu.SMEM(exposure_meta.shape, jnp.int32),
                    pltpu.SMEM(slot_counts.shape, jnp.int32),
                    pltpu.SemaphoreType.DMA((3,)),
                ],
                compiler_params=pltpu.CompilerParams(vmem_limit_bytes=SMALL_VMEM_LIMIT),
                cost_estimate=pl.CostEstimate(flops=ORDER_FLOPS, bytes_accessed=10**6, transcendentals=0),
            )(
                *(
                    pltpu.with_memory_space_constraint(x, pltpu.HBM)
                    for x in (exposure_meta, slot_counts, sed_weights.T)
                ),
                whole,
            )
            after = plans[0]
        own_rows, spill = pl.pallas_call(
            functools.partial(exposures_kernel, terms),
            out_shape=(
                jax.ShapeDtypeStruct(whole_shape, jnp.float32),
                jax.ShapeDtypeStruct(rim_shape, jnp.bfloat16),
            ),
            in_specs=[smem] * 2 + [vmem] * 9,
            out_specs=(vmem, vmem),
            scratch_shapes=[
                pltpu.VMEM((bands, region_rows + rim_rows, win_cols), jnp.bfloat16),
                pltpu.VMEM((bands, region_rows + rim_rows, win_cols), jnp.float32),
            ],
            compiler_params=pltpu.CompilerParams(vmem_limit_bytes=VMEM_LIMIT),
            cost_estimate=pl.CostEstimate(flops=6 * 10**9, bytes_accessed=6 * 10**6, transcendentals=0),
        )(plans[c], sed, whole, following, *prepared[:7])
        spilled = passed_along(spill, "region", 1)
        total, *given = pl.pallas_call(
            share_kernel,
            out_shape=(jax.ShapeDtypeStruct(tile_shape, jnp.float32),)
            + (jax.ShapeDtypeStruct(tile_shape, jnp.bfloat16),) * (shard_count - 1),
            in_specs=[vmem] * 2,
            out_specs=(vmem,) * shard_count,
            compiler_params=pltpu.CompilerParams(vmem_limit_bytes=SMALL_VMEM_LIMIT),
            cost_estimate=pl.CostEstimate(flops=10**5, bytes_accessed=10**6, transcendentals=0),
        )(own_rows, spilled)
        for step in range(1, shard_count):
            total = total + shifted(given[step - 1], "shard", step).astype(jnp.float32)
        result.append(total)
    return jnp.concatenate(result, axis=2)


def solution(mesh):
    placed = (
        P(None, ("region", "shard"), None),
        P(),
        P(),
        P(("region", "shard"), None, None),
        P(("region", "shard"), None, None),
        P(("region", "shard"), None, None),
        P(None, "region"),
        P("region", None),
    )
    return jax.shard_map(
        local,
        mesh=mesh,
        in_specs=placed,
        out_specs=P(None, ("region", "shard"), None),
        check_vma=False,
    )
```

```python
import functools

import jax
import jax.numpy as jnp
from jax import lax
from jax.experimental import pallas as pl
from jax.experimental.pallas import tpu as pltpu
from jax.sharding import PartitionSpec as P

GROUPS = (12, 16, 20)
ROW_ALIGN = 32
ORDER_FLOPS = 10**10
VMEM_LIMIT = 16 * 1024 * 1024
SMALL_VMEM_LIMIT = 4 * 1024 * 1024


def shifted(block, axis, distance):
    size = lax.axis_size(axis)
    return lax.ppermute(block, axis, [(i, (i + distance) % size) for i in range(size)])


def dot(a, b, contract):
    return lax.dot_general(a, b, ((contract[:1], contract[1:]), ((), ())), preferred_element_type=jnp.float32)


def prepare_kernel(
    taps_hbm,
    ry_hbm,
    rx_hbm,
    obs_hbm,
    py_ref,
    py_t_ref,
    px_ref,
    px_t_ref,
    ry_ref,
    rx_ref,
    obs_ref,
    taps_ref,
    lines_ref,
    sems,
):
    bands, terms, axes, tap_count = taps_ref.shape
    half = tap_count // 2
    moves = [
        pltpu.make_async_copy(source, target, sems.at[i])
        for i, (source, target) in enumerate(
            (
                (taps_hbm, taps_ref),
                (ry_hbm, ry_ref),
                (rx_hbm, rx_ref),
                (obs_hbm, obs_ref),
            )
        )
    ]
    for move in moves:
        move.start()
    lines_ref[...] = jnp.zeros_like(lines_ref)
    lanes = lines_ref.shape[2]
    mirror = lax.broadcasted_iota(jnp.int32, (lanes, lanes), 0) + lax.broadcasted_iota(jnp.int32, (lanes, lanes), 1)
    mirror = (mirror == tap_count - 1).astype(jnp.bfloat16)
    moves[0].wait()

    def one_band(b, carry):
        for t in range(terms):
            lines_ref[b, axes * t : axes * (t + 1), :tap_count] = taps_ref[b, t]
        forward = lines_ref[b].astype(jnp.bfloat16)
        mirrored = dot(forward, mirror, (1, 0))
        forward = forward.astype(jnp.float32)
        for axis, (turned_ref, straight_ref) in enumerate(((py_ref, py_t_ref), (px_ref, px_t_ref))):
            width = straight_ref.shape[1]
            down = lax.broadcasted_iota(jnp.int32, (width, width), 0)
            right = lax.broadcasted_iota(jnp.int32, (width, width), 1)
            near = jnp.abs(down - right) <= half
            for lines, out_ref in ((forward, straight_ref), (mirrored, turned_ref)):
                if width > lanes:
                    lines = jnp.concatenate([lines, jnp.zeros((lines.shape[0], width - lanes), jnp.float32)], axis=1)
                centred = pltpu.roll(lines, width - half, 1)
                for t in range(terms):
                    line = centred[axes * t + axis : axes * t + axis + 1]
                    rolled = pltpu.roll(jnp.broadcast_to(line, (width, width)), 0, 1, stride=1, stride_axis=0)
                    table = jnp.where(near, rolled, 0.0)
                    out_ref[b, :, t * width : (t + 1) * width] = table.astype(jnp.bfloat16)
        return carry

    lax.fori_loop(0, bands, one_band, 0, unroll=True)
    for move in moves[1:]:
        move.wait()


def order_kernel(tile_rows, meta_hbm, counts_hbm, sed_hbm, _, sed_ref, *rest):
    plans, (meta_ref, counts_ref, sems) = rest[:-3], rest[-3:]
    slots = (plans[0].shape[0] - 1) // 3
    moves = [
        pltpu.make_async_copy(source, target, sems.at[i])
        for i, (source, target) in enumerate(((meta_hbm, meta_ref), (counts_hbm, counts_ref), (sed_hbm, sed_ref)))
    ]
    for move in moves:
        move.start()
    for move in moves:
        move.wait()
    mine = lax.axis_index("shard")

    def place(slot, found):
        at = mine * slots + slot
        col = meta_ref[1, at]
        after = []
        for c, plan_ref in enumerate(plans):
            plan_ref[1 + found[c]] = slot
            plan_ref[1 + slots + found[c]] = meta_ref[0, at] * tile_rows
            plan_ref[1 + 2 * slots + found[c]] = meta_ref[2, at]
            after.append(found[c] + (col == c).astype(jnp.int32))
        return tuple(after)

    found = lax.fori_loop(0, counts_ref[0, mine], place, (jnp.int32(0),) * len(plans))
    for plan_ref, total in zip(plans, found):
        plan_ref[0] = total


def gather_kernel(*refs):
    tiles, (_, whole_ref, rim_ref) = refs[:-3], refs[-3:]
    count = len(tiles)
    tile_rows = tiles[0].shape[1]
    rim_tiles = rim_ref.shape[1] // tile_rows
    for k in range(count):
        owner = lax.rem(lax.axis_index("shard") + (count - k), count)
        place = pl.ds(pl.multiple_of(owner * tile_rows, tile_rows), tile_rows)
        whole_ref[:, place, :] = tiles[k][...]

        @pl.when(owner < rim_tiles)
        def _(place=place, tile=tiles[k]):
            rim_ref[:, place, :] = tile[...]


def exposures_kernel(
    terms,
    regions,
    plan_ref,
    sed_ref,
    whole_ref,
    next_ref,
    py_ref,
    py_t_ref,
    px_ref,
    px_t_ref,
    ry_ref,
    rx_ref,
    obs_ref,
    own_ref,
    spill_ref,
    mix_ref,
    acc_ref,
):
    channels, bands = sed_ref.shape
    region_rows = whole_ref.shape[1]
    rim_rows = next_ref.shape[1]
    slots, _, win_rows = ry_ref.shape
    win_cols = rx_ref.shape[2]
    count = plan_ref[0]
    acc_ref[...] = jnp.zeros_like(acc_ref)

    has_next = (lax.axis_index("region") < regions - 1).astype(jnp.float32)

    def mix(b, carry):
        for part_ref, start, share in ((whole_ref, 0, None), (next_ref, region_rows, has_next)):
            total = None
            for k in range(channels):
                weight = sed_ref[k, b] if share is None else sed_ref[k, b] * share
                term = weight * part_ref[k].astype(jnp.float32)
                total = term if total is None else total + term
            mix_ref[b, start : start + part_ref.shape[1], :] = total.astype(jnp.bfloat16)
        return carry

    lax.fori_loop(0, bands, mix, 0)

    def visit(group, first):
        members = range(group)
        live = [first + m < count for m in members]
        rank = [jnp.minimum(first + m, count - 1) for m in members]
        slot_of = [plan_ref[1 + r] for r in rank]
        row = [pl.multiple_of(plan_ref[1 + slots + r], ROW_ALIGN) for r in rank]
        band = [plan_ref[1 + 2 * slots + r] for r in rank]
        mixed = [mix_ref[band[m], pl.ds(row[m], win_rows), :] for m in members]
        along = [dot(mixed[m], px_t_ref[band[m]], (1, 0)).astype(jnp.bfloat16) for m in members]
        stack = [
            jnp.concatenate([along[m][:, t * win_cols : (t + 1) * win_cols] for t in range(terms)], axis=0)
            for m in members
        ]
        blurred = [dot(py_ref[band[m]], stack[m], (1, 0)).astype(jnp.bfloat16) for m in members]
        sampled = [dot(ry_ref[slot_of[m]], blurred[m], (1, 0)).astype(jnp.bfloat16) for m in members]
        model = [dot(sampled[m], rx_ref[slot_of[m]], (1, 1)) for m in members]
        misfit = [(model[m] - obs_ref[slot_of[m]].astype(jnp.float32)).astype(jnp.bfloat16) for m in members]
        back_rows = [dot(ry_ref[slot_of[m]], misfit[m], (0, 0)).astype(jnp.bfloat16) for m in members]
        back = [dot(back_rows[m], rx_ref[slot_of[m]], (1, 0)).astype(jnp.bfloat16) for m in members]
        spread = [dot(back[m], px_ref[band[m]], (1, 0)).astype(jnp.bfloat16) for m in members]
        back_along = [
            jnp.concatenate([spread[m][:, t * win_cols : (t + 1) * win_cols] for t in range(terms)], axis=0)
            for m in members
        ]
        window_grad = [dot(py_t_ref[band[m]], back_along[m], (1, 0)) for m in members]
        for m in members:
            place = (band[m], pl.ds(row[m], win_rows), slice(None))
            acc_ref[place] = acc_ref[place] + jnp.where(live[m], window_grad[m], 0.0)

    turns = (count + GROUPS[-1] - 1) // GROUPS[-1]
    fits = [turns * group >= count for group in GROUPS]
    for at, group in enumerate(GROUPS):
        taken = jnp.logical_and(fits[at], jnp.logical_not(fits[at - 1])) if at else fits[at]

        def turn(i, carry, group=group):
            visit(group, i * group)
            return carry

        lax.fori_loop(0, jnp.where(taken, turns, 0), turn, 0)

    for k in range(channels):
        for out_ref, start, rows in ((spill_ref, region_rows, rim_rows), (own_ref, 0, region_rows)):
            total = None
            for b in range(bands):
                term = sed_ref[k, b] * acc_ref[b, start : start + rows, :]
                total = term if total is None else total + term
            out_ref[k] = total.astype(out_ref.dtype)


def share_kernel(own_ref, spilled_ref, kept_ref, *given):
    count = 1 + len(given)
    tile_rows = kept_ref.shape[1]
    rim_tiles = spilled_ref.shape[1] // tile_rows
    for k, out_ref in enumerate((kept_ref,) + given):
        owner = lax.rem(lax.axis_index("shard") + k, count)
        tile = own_ref[:, pl.ds(pl.multiple_of(owner * tile_rows, tile_rows), tile_rows), :]
        rim = pl.ds(pl.multiple_of(jnp.minimum(owner, rim_tiles - 1) * tile_rows, tile_rows), tile_rows)
        takes = jnp.logical_and(owner < rim_tiles, lax.axis_index("region") > 0)
        extra = jnp.where(takes, spilled_ref[:, rim, :].astype(jnp.float32), 0.0)
        out_ref[...] = (tile + extra).astype(out_ref.dtype)


def local(
    planes,
    sed_weights,
    psf_taps,
    resample_rows,
    resample_cols,
    observed,
    exposure_meta,
    slot_counts,
):
    shard_count = lax.axis_size("shard")
    channel_count, tile_rows, col_total = planes.shape
    slot_count, out_rows, win_rows = resample_rows.shape
    win_cols = resample_cols.shape[2]
    col_tiles = col_total // win_cols
    region_rows = tile_rows * shard_count
    rim_rows = win_rows - tile_rows
    bands, terms, tap_count = psf_taps.shape[1:]
    smem = pl.BlockSpec(memory_space=pltpu.SMEM)
    vmem = pl.BlockSpec(memory_space=pltpu.VMEM)
    anywhere = pl.BlockSpec(memory_space=pl.ANY)
    tile_shape = (channel_count, tile_rows, win_cols)
    whole_shape = (channel_count, region_rows, win_cols)
    rim_shape = (channel_count, rim_rows, win_cols)

    tiles = []
    for c in range(col_tiles):
        own = planes[:, :, c * win_cols : (c + 1) * win_cols]
        tiles.append([own] + [shifted(own, "shard", k) for k in range(1, shard_count)])

    def spec(*shape):
        return jax.ShapeDtypeStruct(shape, jnp.bfloat16)

    prepared = pl.pallas_call(
        prepare_kernel,
        out_shape=(
            spec(bands, win_rows, terms * win_rows),
            spec(bands, win_rows, terms * win_rows),
            spec(bands, win_cols, terms * win_cols),
            spec(bands, win_cols, terms * win_cols),
            spec(*resample_rows.shape),
            spec(*resample_cols.shape),
            spec(*observed.shape),
        ),
        in_specs=[anywhere] * 4,
        out_specs=(vmem,) * 7,
        scratch_shapes=[
            pltpu.VMEM((bands, terms, 2, tap_count), jnp.float32),
            pltpu.VMEM((bands, 8 * ((2 * terms + 7) // 8), 128), jnp.float32),
            pltpu.SemaphoreType.DMA((4,)),
        ],
        compiler_params=pltpu.CompilerParams(vmem_limit_bytes=VMEM_LIMIT),
        cost_estimate=pl.CostEstimate(flops=10**8, bytes_accessed=8 * 10**6, transcendentals=0),
    )(
        *(
            pltpu.with_memory_space_constraint(x, pltpu.HBM)
            for x in (psf_taps.transpose(1, 2, 0, 3), resample_rows, resample_cols, observed)
        )
    )

    result = []
    after = prepared[0]
    for c in range(col_tiles):
        whole, rim = pl.pallas_call(
            gather_kernel,
            out_shape=(
                jax.ShapeDtypeStruct(whole_shape, planes.dtype),
                jax.ShapeDtypeStruct(rim_shape, planes.dtype),
            ),
            in_specs=[vmem] * shard_count + [anywhere],
            out_specs=(vmem, vmem),
            compiler_params=pltpu.CompilerParams(vmem_limit_bytes=SMALL_VMEM_LIMIT),
            cost_estimate=pl.CostEstimate(flops=10**5, bytes_accessed=10**6, transcendentals=0),
        )(*tiles[c], after)
        following = shifted(rim, "region", -1)
        if c == 0:
            sed, *plans = pl.pallas_call(
                functools.partial(order_kernel, tile_rows),
                out_shape=(jax.ShapeDtypeStruct(sed_weights.shape[::-1], jnp.float32),)
                + (jax.ShapeDtypeStruct((1 + 3 * slot_count,), jnp.int32),) * col_tiles,
                in_specs=[anywhere] * 4,
                out_specs=(smem,) * (1 + col_tiles),
                scratch_shapes=[
                    pltpu.SMEM(exposure_meta.shape, jnp.int32),
                    pltpu.SMEM(slot_counts.shape, jnp.int32),
                    pltpu.SemaphoreType.DMA((3,)),
                ],
                compiler_params=pltpu.CompilerParams(vmem_limit_bytes=SMALL_VMEM_LIMIT),
                cost_estimate=pl.CostEstimate(flops=ORDER_FLOPS, bytes_accessed=10**6, transcendentals=0),
            )(
                *(
                    pltpu.with_memory_space_constraint(x, pltpu.HBM)
                    for x in (exposure_meta, slot_counts, sed_weights.T)
                ),
                whole,
            )
            after = plans[0]
        own_rows, spill = pl.pallas_call(
            functools.partial(exposures_kernel, terms, lax.axis_size("region")),
            out_shape=(
                jax.ShapeDtypeStruct(whole_shape, jnp.float32),
                jax.ShapeDtypeStruct(rim_shape, jnp.bfloat16),
            ),
            in_specs=[smem] * 2 + [vmem] * 9,
            out_specs=(vmem, vmem),
            scratch_shapes=[
                pltpu.VMEM((bands, region_rows + rim_rows, win_cols), jnp.bfloat16),
                pltpu.VMEM((bands, region_rows + rim_rows, win_cols), jnp.float32),
            ],
            compiler_params=pltpu.CompilerParams(vmem_limit_bytes=VMEM_LIMIT),
            cost_estimate=pl.CostEstimate(flops=6 * 10**9, bytes_accessed=6 * 10**6, transcendentals=0),
        )(plans[c], sed, whole, following, *prepared[:7])
        spilled = shifted(spill, "region", 1)
        total, *given = pl.pallas_call(
            share_kernel,
            out_shape=(jax.ShapeDtypeStruct(tile_shape, jnp.float32),)
            + (jax.ShapeDtypeStruct(tile_shape, jnp.bfloat16),) * (shard_count - 1),
            in_specs=[vmem] * 2,
            out_specs=(vmem,) * shard_count,
            compiler_params=pltpu.CompilerParams(vmem_limit_bytes=SMALL_VMEM_LIMIT),
            cost_estimate=pl.CostEstimate(flops=10**5, bytes_accessed=10**6, transcendentals=0),
        )(own_rows, spilled)
        for step in range(1, shard_count):
            total = total + shifted(given[step - 1], "shard", step).astype(jnp.float32)
        result.append(total)
    return jnp.concatenate(result, axis=2)


def solution(mesh):
    placed = (
        P(None, ("region", "shard"), None),
        P(),
        P(),
        P(("region", "shard"), None, None),
        P(("region", "shard"), None, None),
        P(("region", "shard"), None, None),
        P(None, "region"),
        P("region", None),
    )
    return jax.shard_map(
        local,
        mesh=mesh,
        in_specs=placed,
        out_specs=P(None, ("region", "shard"), None),
        check_vma=False,
    )
```

```python
import functools

import jax
import jax.numpy as jnp
from jax import lax
from jax.experimental import pallas as pl
from jax.experimental.pallas import tpu as pltpu
from jax.sharding import PartitionSpec as P

GROUPS = (12, 16, 20)
ROW_ALIGN = 32
UNROLL = 2
ORDER_FLOPS = 10**10
VMEM_LIMIT = 16 * 1024 * 1024
SMALL_VMEM_LIMIT = 4 * 1024 * 1024


def shifted(block, axis, distance):
    size = lax.axis_size(axis)
    return lax.ppermute(block, axis, [(i, (i + distance) % size) for i in range(size)])


def dot(a, b, contract):
    return lax.dot_general(a, b, ((contract[:1], contract[1:]), ((), ())), preferred_element_type=jnp.float32)


def prepare_kernel(
    taps_hbm,
    ry_hbm,
    rx_hbm,
    obs_hbm,
    py_ref,
    py_t_ref,
    px_ref,
    px_t_ref,
    ry_ref,
    rx_ref,
    obs_ref,
    taps_ref,
    lines_ref,
    sems,
):
    bands, terms, axes, tap_count = taps_ref.shape
    half = tap_count // 2
    moves = [
        pltpu.make_async_copy(source, target, sems.at[i])
        for i, (source, target) in enumerate(
            (
                (taps_hbm, taps_ref),
                (ry_hbm, ry_ref),
                (rx_hbm, rx_ref),
                (obs_hbm, obs_ref),
            )
        )
    ]
    for move in moves:
        move.start()
    lines_ref[...] = jnp.zeros_like(lines_ref)
    lanes = lines_ref.shape[2]
    mirror = lax.broadcasted_iota(jnp.int32, (lanes, lanes), 0) + lax.broadcasted_iota(jnp.int32, (lanes, lanes), 1)
    mirror = (mirror == tap_count - 1).astype(jnp.bfloat16)
    moves[0].wait()

    def one_band(b, carry):
        for t in range(terms):
            lines_ref[b, axes * t : axes * (t + 1), :tap_count] = taps_ref[b, t]
        forward = lines_ref[b].astype(jnp.bfloat16)
        mirrored = dot(forward, mirror, (1, 0))
        forward = forward.astype(jnp.float32)
        for axis, (turned_ref, straight_ref) in enumerate(((py_ref, py_t_ref), (px_ref, px_t_ref))):
            width = straight_ref.shape[1]
            down = lax.broadcasted_iota(jnp.int32, (width, width), 0)
            right = lax.broadcasted_iota(jnp.int32, (width, width), 1)
            near = jnp.abs(down - right) <= half
            for lines, out_ref in ((forward, straight_ref), (mirrored, turned_ref)):
                if width > lanes:
                    lines = jnp.concatenate([lines, jnp.zeros((lines.shape[0], width - lanes), jnp.float32)], axis=1)
                centred = pltpu.roll(lines, width - half, 1)
                for t in range(terms):
                    line = centred[axes * t + axis : axes * t + axis + 1]
                    rolled = pltpu.roll(jnp.broadcast_to(line, (width, width)), 0, 1, stride=1, stride_axis=0)
                    table = jnp.where(near, rolled, 0.0)
                    out_ref[b, :, t * width : (t + 1) * width] = table.astype(jnp.bfloat16)
        return carry

    lax.fori_loop(0, bands, one_band, 0, unroll=True)
    for move in moves[1:]:
        move.wait()


def order_kernel(tile_rows, meta_hbm, counts_hbm, sed_hbm, _, sed_ref, *rest):
    plans, (meta_ref, counts_ref, sems) = rest[:-3], rest[-3:]
    slots = (plans[0].shape[0] - 1) // 3
    moves = [
        pltpu.make_async_copy(source, target, sems.at[i])
        for i, (source, target) in enumerate(((meta_hbm, meta_ref), (counts_hbm, counts_ref), (sed_hbm, sed_ref)))
    ]
    for move in moves:
        move.start()
    for move in moves:
        move.wait()
    mine = lax.axis_index("shard")

    def place(slot, found):
        at = mine * slots + slot
        col = meta_ref[1, at]
        after = []
        for c, plan_ref in enumerate(plans):
            plan_ref[1 + found[c]] = slot
            plan_ref[1 + slots + found[c]] = meta_ref[0, at] * tile_rows
            plan_ref[1 + 2 * slots + found[c]] = meta_ref[2, at]
            after.append(found[c] + (col == c).astype(jnp.int32))
        return tuple(after)

    found = lax.fori_loop(0, counts_ref[0, mine], place, (jnp.int32(0),) * len(plans))
    for plan_ref, total in zip(plans, found):
        plan_ref[0] = total


def gather_kernel(*refs):
    tiles, (_, whole_ref, rim_ref) = refs[:-3], refs[-3:]
    count = len(tiles)
    tile_rows = tiles[0].shape[1]
    rim_tiles = rim_ref.shape[1] // tile_rows
    for k in range(count):
        owner = lax.rem(lax.axis_index("shard") + (count - k), count)
        place = pl.ds(pl.multiple_of(owner * tile_rows, tile_rows), tile_rows)
        whole_ref[:, place, :] = tiles[k][...]

        @pl.when(owner < rim_tiles)
        def _(place=place, tile=tiles[k]):
            rim_ref[:, place, :] = tile[...]


def mixed_planes(sed_ref, part_ref, b, share):
    total = None
    for k in range(part_ref.shape[0]):
        weight = sed_ref[k, b] if share is None else sed_ref[k, b] * share
        term = weight * part_ref[k].astype(jnp.float32)
        total = term if total is None else total + term
    return total.astype(jnp.bfloat16)


def mix_planes(sed_ref, part_ref, mix_ref, start, share=None):
    def one_band(b, carry):
        mix_ref[b, start : start + part_ref.shape[1], :] = mixed_planes(sed_ref, part_ref, b, share)
        return carry

    lax.fori_loop(0, sed_ref.shape[1], one_band, 0)


def blur_columns(sed_ref, part_ref, px_t_ref, wide_ref, start, share=None):
    rows = part_ref.shape[1]
    terms, cols = wide_ref.shape[1], wide_ref.shape[3]

    def one_band(b, carry):
        along = dot(mixed_planes(sed_ref, part_ref, b, share), px_t_ref[b], (1, 0)).astype(jnp.bfloat16)
        for t in range(terms):
            wide_ref[b, t, start : start + rows, :] = along[:, t * cols : (t + 1) * cols]
        return carry

    lax.fori_loop(0, sed_ref.shape[1], one_band, 0, unroll=UNROLL)


def blur_kernel(sed_ref, whole_ref, px_t_ref, wide_ref):
    blur_columns(sed_ref, whole_ref, px_t_ref, wide_ref, 0)


def exposures_kernel(
    terms,
    regions,
    ready,
    plan_ref,
    sed_ref,
    whole_ref,
    next_ref,
    py_ref,
    py_t_ref,
    px_ref,
    px_t_ref,
    ry_ref,
    rx_ref,
    obs_ref,
    own_ref,
    spill_ref,
    wide_ref,
    acc_ref,
):
    channels, bands = sed_ref.shape
    region_rows = own_ref.shape[1]
    rim_rows = next_ref.shape[1]
    slots, _, win_rows = ry_ref.shape
    win_cols = rx_ref.shape[2]
    count = plan_ref[0]
    acc_ref[...] = jnp.zeros_like(acc_ref)
    has_next = (lax.axis_index("region") < regions - 1).astype(jnp.float32)
    if ready:
        wide_ref[:, :, :region_rows, :] = whole_ref[...]
        blur_columns(sed_ref, next_ref, px_t_ref, wide_ref, region_rows, has_next)
    else:
        mix_planes(sed_ref, whole_ref, wide_ref, 0)
        mix_planes(sed_ref, next_ref, wide_ref, region_rows, has_next)

    def visit(group, first):
        members = range(group)
        live = [first + m < count for m in members]
        rank = [jnp.minimum(first + m, count - 1) for m in members]
        slot_of = [plan_ref[1 + r] for r in rank]
        row = [pl.multiple_of(plan_ref[1 + slots + r], ROW_ALIGN) for r in rank]
        band = [plan_ref[1 + 2 * slots + r] for r in rank]
        window = [pl.ds(r, win_rows) for r in row]
        if ready:
            along = [[wide_ref[band[m], t, window[m], :] for t in range(terms)] for m in members]
        else:
            mixed = [wide_ref[band[m], window[m], :] for m in members]
            joined = [dot(mixed[m], px_t_ref[band[m]], (1, 0)).astype(jnp.bfloat16) for m in members]
            along = [[joined[m][:, t * win_cols : (t + 1) * win_cols] for t in range(terms)] for m in members]
        stack = [jnp.concatenate(along[m], axis=0) for m in members]
        blurred = [dot(py_ref[band[m]], stack[m], (1, 0)).astype(jnp.bfloat16) for m in members]
        sampled = [dot(ry_ref[slot_of[m]], blurred[m], (1, 0)).astype(jnp.bfloat16) for m in members]
        model = [dot(sampled[m], rx_ref[slot_of[m]], (1, 1)) for m in members]
        misfit = [(model[m] - obs_ref[slot_of[m]].astype(jnp.float32)).astype(jnp.bfloat16) for m in members]
        back_rows = [dot(ry_ref[slot_of[m]], misfit[m], (0, 0)).astype(jnp.bfloat16) for m in members]
        back = [dot(back_rows[m], rx_ref[slot_of[m]], (1, 0)).astype(jnp.bfloat16) for m in members]
        spread = [dot(back[m], px_ref[band[m]], (1, 0)).astype(jnp.bfloat16) for m in members]
        back_along = [
            jnp.concatenate([spread[m][:, t * win_cols : (t + 1) * win_cols] for t in range(terms)], axis=0)
            for m in members
        ]
        window_grad = [dot(py_t_ref[band[m]], back_along[m], (1, 0)) for m in members]
        for m in members:
            place = (band[m], pl.ds(row[m], win_rows), slice(None))
            acc_ref[place] = acc_ref[place] + jnp.where(live[m], window_grad[m], 0.0)

    turns = (count + GROUPS[-1] - 1) // GROUPS[-1]
    fits = [turns * group >= count for group in GROUPS]
    for at, group in enumerate(GROUPS):
        taken = jnp.logical_and(fits[at], jnp.logical_not(fits[at - 1])) if at else fits[at]

        def turn(i, carry, group=group):
            visit(group, i * group)
            return carry

        lax.fori_loop(0, jnp.where(taken, turns, 0), turn, 0)

    for k in range(channels):
        for out_ref, start, rows in ((spill_ref, region_rows, rim_rows), (own_ref, 0, region_rows)):
            total = None
            for b in range(bands):
                term = sed_ref[k, b] * acc_ref[b, start : start + rows, :]
                total = term if total is None else total + term
            out_ref[k] = total.astype(out_ref.dtype)


def share_kernel(own_ref, spilled_ref, kept_ref, *given):
    count = 1 + len(given)
    tile_rows = kept_ref.shape[1]
    rim_tiles = spilled_ref.shape[1] // tile_rows
    for k, out_ref in enumerate((kept_ref,) + given):
        owner = lax.rem(lax.axis_index("shard") + k, count)
        tile = own_ref[:, pl.ds(pl.multiple_of(owner * tile_rows, tile_rows), tile_rows), :]
        rim = pl.ds(pl.multiple_of(jnp.minimum(owner, rim_tiles - 1) * tile_rows, tile_rows), tile_rows)
        takes = jnp.logical_and(owner < rim_tiles, lax.axis_index("region") > 0)
        extra = jnp.where(takes, spilled_ref[:, rim, :].astype(jnp.float32), 0.0)
        out_ref[...] = (tile + extra).astype(out_ref.dtype)


def local(
    planes,
    sed_weights,
    psf_taps,
    resample_rows,
    resample_cols,
    observed,
    exposure_meta,
    slot_counts,
):
    shard_count = lax.axis_size("shard")
    channel_count, tile_rows, col_total = planes.shape
    slot_count, out_rows, win_rows = resample_rows.shape
    win_cols = resample_cols.shape[2]
    col_tiles = col_total // win_cols
    region_rows = tile_rows * shard_count
    rim_rows = win_rows - tile_rows
    bands, terms, tap_count = psf_taps.shape[1:]
    smem = pl.BlockSpec(memory_space=pltpu.SMEM)
    vmem = pl.BlockSpec(memory_space=pltpu.VMEM)
    anywhere = pl.BlockSpec(memory_space=pl.ANY)
    tile_shape = (channel_count, tile_rows, win_cols)
    whole_shape = (channel_count, region_rows, win_cols)
    rim_shape = (channel_count, rim_rows, win_cols)

    tiles = []
    for c in range(col_tiles):
        own = planes[:, :, c * win_cols : (c + 1) * win_cols]
        tiles.append([own] + [shifted(own, "shard", k) for k in range(1, shard_count)])

    def spec(*shape):
        return jax.ShapeDtypeStruct(shape, jnp.bfloat16)

    prepared = pl.pallas_call(
        prepare_kernel,
        out_shape=(
            spec(bands, win_rows, terms * win_rows),
            spec(bands, win_rows, terms * win_rows),
            spec(bands, win_cols, terms * win_cols),
            spec(bands, win_cols, terms * win_cols),
            spec(*resample_rows.shape),
            spec(*resample_cols.shape),
            spec(*observed.shape),
        ),
        in_specs=[anywhere] * 4,
        out_specs=(vmem,) * 7,
        scratch_shapes=[
            pltpu.VMEM((bands, terms, 2, tap_count), jnp.float32),
            pltpu.VMEM((bands, 8 * ((2 * terms + 7) // 8), 128), jnp.float32),
            pltpu.SemaphoreType.DMA((4,)),
        ],
        compiler_params=pltpu.CompilerParams(vmem_limit_bytes=VMEM_LIMIT),
        cost_estimate=pl.CostEstimate(flops=10**8, bytes_accessed=8 * 10**6, transcendentals=0),
    )(
        *(
            pltpu.with_memory_space_constraint(x, pltpu.HBM)
            for x in (psf_taps.transpose(1, 2, 0, 3), resample_rows, resample_cols, observed)
        )
    )

    result = []
    after = prepared[0]
    for c in range(col_tiles):
        whole, rim = pl.pallas_call(
            gather_kernel,
            out_shape=(
                jax.ShapeDtypeStruct(whole_shape, planes.dtype),
                jax.ShapeDtypeStruct(rim_shape, planes.dtype),
            ),
            in_specs=[vmem] * shard_count + [anywhere],
            out_specs=(vmem, vmem),
            compiler_params=pltpu.CompilerParams(vmem_limit_bytes=SMALL_VMEM_LIMIT),
            cost_estimate=pl.CostEstimate(flops=10**5, bytes_accessed=10**6, transcendentals=0),
        )(*tiles[c], after)
        following = shifted(rim, "region", -1)
        if c == 0:
            sed, *plans = pl.pallas_call(
                functools.partial(order_kernel, tile_rows),
                out_shape=(jax.ShapeDtypeStruct(sed_weights.shape[::-1], jnp.float32),)
                + (jax.ShapeDtypeStruct((1 + 3 * slot_count,), jnp.int32),) * col_tiles,
                in_specs=[anywhere] * 4,
                out_specs=(smem,) * (1 + col_tiles),
                scratch_shapes=[
                    pltpu.SMEM(exposure_meta.shape, jnp.int32),
                    pltpu.SMEM(slot_counts.shape, jnp.int32),
                    pltpu.SemaphoreType.DMA((3,)),
                ],
                compiler_params=pltpu.CompilerParams(vmem_limit_bytes=SMALL_VMEM_LIMIT),
                cost_estimate=pl.CostEstimate(flops=ORDER_FLOPS, bytes_accessed=10**6, transcendentals=0),
            )(
                *(
                    pltpu.with_memory_space_constraint(x, pltpu.HBM)
                    for x in (exposure_meta, slot_counts, sed_weights.T)
                ),
                whole,
            )
            after = plans[0]
            whole = pl.pallas_call(
                blur_kernel,
                out_shape=spec(bands, terms, region_rows, win_cols),
                in_specs=[smem] + [vmem] * 2,
                out_specs=vmem,
                compiler_params=pltpu.CompilerParams(vmem_limit_bytes=SMALL_VMEM_LIMIT),
                cost_estimate=pl.CostEstimate(flops=10**9, bytes_accessed=10**6, transcendentals=0),
            )(sed, whole, prepared[3])
            after = whole
        own_rows, spill = pl.pallas_call(
            functools.partial(exposures_kernel, terms, lax.axis_size("region"), c == 0),
            out_shape=(
                jax.ShapeDtypeStruct(whole_shape, jnp.float32),
                jax.ShapeDtypeStruct(rim_shape, jnp.bfloat16),
            ),
            in_specs=[smem] * 2 + [vmem] * 9,
            out_specs=(vmem, vmem),
            scratch_shapes=[
                pltpu.VMEM((bands,) + ((terms,) if c == 0 else ()) + (region_rows + rim_rows, win_cols), jnp.bfloat16),
                pltpu.VMEM((bands, region_rows + rim_rows, win_cols), jnp.float32),
            ],
            compiler_params=pltpu.CompilerParams(vmem_limit_bytes=VMEM_LIMIT),
            cost_estimate=pl.CostEstimate(flops=6 * 10**9, bytes_accessed=6 * 10**6, transcendentals=0),
        )(plans[c], sed, whole, following, *prepared[:7])
        spilled = shifted(spill, "region", 1)
        total, *given = pl.pallas_call(
            share_kernel,
            out_shape=(jax.ShapeDtypeStruct(tile_shape, jnp.float32),)
            + (jax.ShapeDtypeStruct(tile_shape, jnp.bfloat16),) * (shard_count - 1),
            in_specs=[vmem] * 2,
            out_specs=(vmem,) * shard_count,
            compiler_params=pltpu.CompilerParams(vmem_limit_bytes=SMALL_VMEM_LIMIT),
            cost_estimate=pl.CostEstimate(flops=10**5, bytes_accessed=10**6, transcendentals=0),
        )(own_rows, spilled)
        for step in range(1, shard_count):
            total = total + shifted(given[step - 1], "shard", step).astype(jnp.float32)
        result.append(total)
    return jnp.concatenate(result, axis=2)


def solution(mesh):
    placed = (
        P(None, ("region", "shard"), None),
        P(),
        P(),
        P(("region", "shard"), None, None),
        P(("region", "shard"), None, None),
        P(("region", "shard"), None, None),
        P(None, "region"),
        P("region", None),
    )
    return jax.shard_map(
        local,
        mesh=mesh,
        in_specs=placed,
        out_specs=P(None, ("region", "shard"), None),
        check_vma=False,
    )
```
